32 devices in a mesh: rep: 8 (over y, x, core), shard: 4 (over z).
Axes of the slice: x: 2, y: 2, z: 4, core: 2. Of those that a mesh axis runs over, the one named last changes fastest.
Arguments:
- grads_matrix: bfloat16 [8, 4, 3, 1024, 1024], P('rep', 'shard'), may hold values from -400 to 400
- grads_vector: bfloat16 [8, 4, 5, 1024], P('rep', 'shard'), may hold values from -6 to 6
- master_matrix: float32 [3, 1024, 1024], P(None, 'shard'), may hold values from -0.1875 to 0.1875
- master_vector: float32 [5, 1024], P(None, 'shard'), may hold values from 0.5 to 1.5
- moment_matrix: float32 [3, 1024, 1024], P(None, 'shard'), may hold values from -4 to 4
- moment_vector: float32 [5, 1024], P(None, 'shard'), may hold values from -4 to 4
- second_matrix: float32 [3, 1024, 1024], P(None, 'shard'), may hold values from 0.05 to 2
- second_vector: float32 [5, 1024], P(None, 'shard'), may hold values from 0.05 to 2
Outputs:
- matrix_master: float32 [3, 1024, 1024], P(None, 'shard')
- vector_master: float32 [5, 1024], P(None, 'shard')
- matrix_moment: float32 [3, 1024, 1024], P(None, 'shard')
- vector_moment: float32 [5, 1024], P(None, 'shard')
- matrix_second: float32 [3, 1024, 1024], P(None, 'shard')
- vector_second: float32 [5, 1024], P(None, 'shard')
- matrix_weights: bfloat16 [3, 1024, 1024], replicated
- vector_weights: bfloat16 [5, 1024], replicated
The draws below stay inside these ranges and needn't reach their ends.
All inputs are finite; a program needn't handle non-finite values.
Results may differ from the reference program's by a relative error of at most 0.005.
Values may be sent and summed in bfloat16 or wider, within the bound.
A program may use at most 128 MiB of HBM per device.

```python
import math
import jax
import jax.numpy as jnp
from jax import lax

D = 1024
STEP = 1000
REPLICAS = 8
GROUP = 4


def draw_grads_matrix(key, part):
    k_row, k_col, k_main = jax.random.split(key, 3)
    position = jnp.arange(D, dtype=jnp.float32) / (D - 1)
    row_scale = jnp.exp(jax.random.uniform(k_row, (3, D, 1), dtype=jnp.float32) * math.log(3.5))
    col_scale = jnp.exp(jax.random.uniform(k_col, (3, 1, D), dtype=jnp.float32) * math.log(10.0))
    shape = (REPLICAS, GROUP, 3, D, D)
    rising = jnp.exp(math.log(3.0) * position)[:, None]
    values = 0.1 * jnp.clip(jax.random.normal(k_main, shape, dtype=jnp.float32), -6.0, 6.0)
    return (values * rising * row_scale * col_scale).astype(jnp.bfloat16)


def strengthened(drawn, rng, source, target, shards_of, factor):
    owner, partner = [(jnp.arange(drawn.shape[dim]) // (drawn.shape[dim] // shards_of)).reshape([-1 if axis == dim else 1 for axis in range(drawn.ndim)]) for dim in (source, target)]
    chosen = jax.random.permutation(rng, shards_of)[partner]
    strong = (owner == chosen) | (owner == (partner + shards_of // 2) % shards_of)
    return jnp.where(strong, factor * drawn, drawn)


def block_levels(key, extent, cuts, least, largest):
    level = 1.0
    for dim, blocks in cuts:
        steps = jax.random.uniform(jax.random.fold_in(jax.random.fold_in(key, 6), dim), (blocks,), jnp.float32, least / len(cuts), largest / len(cuts))
        level = level * jnp.repeat(jnp.exp(steps), extent[dim] // blocks).reshape((-1,) + (1,) * (len(extent) - 1 - dim))
    return level


def bell_draw(stream_key, dims, scale, reach, cuts=(), held_as=jnp.bfloat16):
    loudness = block_levels(stream_key, dims, cuts, -0.22, 0.18) if cuts else 1.0
    drawn = jax.random.normal(stream_key, dims, jnp.float32) * scale * loudness
    return jnp.minimum(jnp.maximum(drawn, -reach), reach).astype(held_as)


def bell_draw_with(key, shape, scale, reach, shards, heavy, kind=jnp.bfloat16):
    values = scale * jax.random.normal(key, shape, jnp.float32)
    if shards:
        values = values * block_levels(key, shape, shards, -0.22, 0.18)
    return jnp.clip(strengthened(values, jax.random.fold_in(key, 3), *heavy), -reach, reach).astype(kind)


def setup_inputs(seed: int = 0) -> dict:
    streams_of = jax.random.split(jax.random.key(seed), 9)
    return {
        "grads_matrix": draw_grads_matrix(jax.random.fold_in(streams_of[8], 71), 0),
        "grads_vector": bell_draw_with(streams_of[1], (REPLICAS, GROUP, 5, D), 0.8, 6.0, ((0, 8), (1, 4)), (1, 3, 4, 2.0)),
        "master_matrix": bell_draw(streams_of[2], (3, D, D), D ** -0.5, 0.1875, ((1, 4),), jnp.float32),
        "master_vector": jnp.clip(1.0 + 0.1 * jax.random.normal(streams_of[3], (5, D), jnp.float32), 0.5, 1.5),
        "moment_matrix": bell_draw(streams_of[4], (3, D, D), 0.3, 4.0, ((1, 4),), jnp.float32),
        "moment_vector": bell_draw(streams_of[5], (5, D), 0.3, 4.0, ((1, 4),), jnp.float32),
        "second_matrix": jnp.clip(jnp.exp(math.log(2.0) - 3.6888794 * jax.random.uniform(streams_of[6], (3, D, D), jnp.float32) ** block_levels(streams_of[6], (3, D, D), ((1, 4),), -0.2, 0.2)), 0.05, 2.0),
        "second_vector": jnp.clip(jnp.exp(math.log(2.0) - 3.6888794 * jax.random.uniform(streams_of[7], (5, D), jnp.float32) ** block_levels(streams_of[7], (5, D), ((1, 4),), -0.2, 0.2)), 0.05, 2.0),
    }


beta_first = 0.9
beta_second = 0.999
learn_rate = 0.01
decay_rate = 0.1
epsilon = 1e-08

def adam_piece(total, master, moment, second, clip, decay):
    scaled = total * clip
    moment_next = beta_first * moment + (1.0 - beta_first) * scaled
    second_next = beta_second * second + (1.0 - beta_second) * scaled * scaled
    corrected = moment_next / (1.0 - beta_first ** STEP)
    spread = jnp.sqrt(second_next / (1.0 - beta_second ** STEP))
    update = corrected / (spread + epsilon)
    master_next = master - learn_rate * (update + decay * master)
    return (master_next, moment_next, second_next)

def reference(grads_matrix, grads_vector, master_matrix, master_vector, moment_matrix, moment_vector, second_matrix, second_vector):

    def add_piece(total, piece):
        return (total + piece.astype(jnp.float32), None)
    stacked = grads_matrix.reshape((REPLICAS * GROUP, 3, D, D))
    total_matrix, unused = lax.scan(add_piece, jnp.zeros((3, D, D), jnp.float32), stacked)
    total_vector = lax.optimization_barrier(jnp.sum(grads_vector.astype(jnp.float32), axis=(0, 1)))
    count = 3 * D * D + 5 * D
    mean_square = (jnp.sum(total_matrix * total_matrix) + jnp.sum(total_vector * total_vector)) / count
    clip = jnp.minimum(1.0, 1.0 / jnp.sqrt(mean_square + 1e-06))
    master_mat, moment_mat, second_mat = adam_piece(total_matrix, master_matrix, moment_matrix, second_matrix, clip, decay_rate)
    master_vec, moment_vec, second_vec = adam_piece(total_vector, master_vector, moment_vector, second_vector, clip, 0.0)
    return (master_mat, master_vec, moment_mat, moment_vec, second_mat, second_vec, master_mat.astype(jnp.bfloat16), master_vec.astype(jnp.bfloat16))
```

```python
import functools
import math

import jax
import jax.numpy as jnp
from jax import lax
from jax.experimental import pallas as pl
from jax.experimental.pallas import tpu as pltpu
from jax.sharding import PartitionSpec as P

STEP = 1000


beta_first = 0.9
beta_second = 0.999
learn_rate = 0.01
decay_rate = 0.1
epsilon = 1e-08

SPLIT = 1


def adam_piece(total, master, moment, second, clip, decay):
    scaled = total * clip
    moment_next = beta_first * moment + (1.0 - beta_first) * scaled
    second_next = beta_second * second + (1.0 - beta_second) * scaled * scaled
    corrected = moment_next / (1.0 - beta_first**STEP)
    spread = jnp.sqrt(second_next / (1.0 - beta_second**STEP))
    update = corrected / (spread + epsilon)
    master_next = master - learn_rate * (update + decay * master)
    return (master_next, moment_next, second_next)


def kernel(
    R, S, count,
    gm, gv, mm, mv, om, ov, sm, sv,
    wout, tot, clip_out, vtot, vecw,
    acc, rC, rX, rZ, wp, wq, vbuf, rV, sq, sqs, rS, vmine,
    bm, bo, bs,
    lsem, csem, xsem, zsem, gsem, vsem, ssem, wzsem, wgsem, wvsem, psem, osem,
):
    f32, bf16 = jnp.float32, jnp.bfloat16
    n = int(math.log2(R))
    M, _, Q, W = gm.shape
    half = W // 2
    cw = half // SPLIT
    K = M * SPLIT
    r = lax.axis_index("rep")
    z = lax.axis_index("shard")
    core = r % 2
    bits, partners = [], []
    for i in range(n - 1):
        lo, hi = 2 << i, 1 << (n - 1 - i)
        mask = lo + core * (hi - lo)
        bit = (1 - core) * ((r // lo) % 2) + core * ((r // hi) % 2)
        bits.append(bit)
        partners.append(r + (1 - 2 * bit) * mask)
    twin = r + 1 - 2 * core
    sizes = [Q >> i for i in range(n)]
    offs = [0]
    for i in range(n - 1):
        offs.append(offs[-1] + bits[i] * sizes[i + 1])
    al = sizes[n - 1]
    pr = sizes[n - 1]

    def mul(x, m):
        return x if isinstance(x, int) else pl.multiple_of(x, m)

    off = [mul(o, al) for o in offs]
    mycol = lambda j: pl.ds(pl.multiple_of(core * half + j * cw, cw), cw)
    otcol = lambda j: pl.ds(pl.multiple_of((1 - core) * half + j * cw, cw), cw)
    myhalf = pl.ds(pl.multiple_of(core * half, half), half)
    zpeer = [lax.rem(z + d, S) for d in range(S)]
    zfrom = [lax.rem(z + S - d, S) for d in range(S)]

    sends = []

    def remote(src, dst, ss, rs, rep=None, shard=None):
        where = {"rep": rep} if shard is None else {"shard": shard}
        cp = pltpu.make_async_remote_copy(
            src_ref=src, dst_ref=dst, send_sem=ss, recv_sem=rs,
            device_id=where, device_id_type=pl.DeviceIdType.MESH,
        )
        cp.start()
        sends.append(cp)
        return cp

    barrier = pltpu.get_barrier_semaphore()
    for p in [twin] + partners:
        pl.semaphore_signal(barrier, inc=1, device_id={"rep": p}, device_id_type=pl.DeviceIdType.MESH)
    for d in range(1, S):
        pl.semaphore_signal(barrier, inc=1, device_id={"shard": zpeer[d]}, device_id_type=pl.DeviceIdType.MESH)

    locs = []
    for k in range(K):
        m, j = k // SPLIT, k % SPLIT
        cp = pltpu.make_async_copy(gm.at[m, :, :, mycol(j)], acc.at[k], lsem.at[k])
        cp.start()
        locs.append(cp)
    vbuf[...] = jnp.zeros_like(vbuf)
    vbuf[0, 0:5, :] = gv[...].astype(f32)
    pl.semaphore_wait(barrier, n + S - 1)

    cC = []
    for k in range(K):
        m, j = k // SPLIT, k % SPLIT
        cC.append(remote(gm.at[m, :, :, otcol(j)], rC.at[k], csem.at[0, k], csem.at[1, k], rep=twin))
    cV = {0: [remote(vbuf.at[0], rV.at[0], vsem.at[0, 0], vsem.at[1, 0], rep=twin)]}
    ins = []
    for i, (a, b) in enumerate(((mm, bm), (om, bo), (sm, bs))):
        cp = pltpu.make_async_copy(a, b, psem.at[i])
        cp.start()
        ins.append(cp)

    def add_rows(k, recv, start, size, base):
        step = min(size, 64)

        @pl.loop(0, S)
        def _(s):
            for b in range(size // step):
                rows = pl.ds(mul(start + b * step, 16), step)
                theirs = pl.ds(mul(start - base + b * step, 16), step)
                acc[k, s, rows, :] = (acc[k, s, rows, :].astype(f32) + recv[s, theirs, :].astype(f32)).astype(bf16)

    cX, cZ, cG = {}, {}, {}
    other = [mul(offs[i] + (1 - bits[i]) * sizes[i + 1], al) for i in range(n - 1)]

    def stage(k, st):
        m, j = k // SPLIT, k % SPLIT
        if st < n:
            if st == 0:
                locs[k].wait()
                cC[k].wait_recv()
                recv, base = rC.at[k], 0
            else:
                cX[k, st - 1].wait_recv()
                recv, base = rX[st - 1].at[k], offs[st]
            if st < n - 1:
                add_rows(k, recv, other[st], sizes[st + 1], base)
                cX[k, st] = remote(
                    acc.at[k, :, pl.ds(other[st], sizes[st + 1]), :], rX[st].at[k],
                    xsem.at[0, k, st], xsem.at[1, k, st], rep=partners[st])
                add_rows(k, recv, off[st + 1], sizes[st + 1], base)
            else:
                add_rows(k, recv, off[st], sizes[st], base)
                for d in range(1, S):
                    cZ[k, d] = remote(
                        acc.at[k, zpeer[d], pl.ds(off[st], pr), :], rZ.at[k, d - 1],
                        zsem.at[0, k, d - 1], zsem.at[1, k, d - 1], shard=zpeer[d])
        elif st == n:
            own = acc[k, z, pl.ds(off[n - 1], pr), :].astype(f32)
            for d in range(1, S):
                cZ[k, d].wait_recv()
                own = own + rZ[k, d - 1].astype(f32)
            tot[m, pl.ds(off[n - 1], pr), mycol(j)] = own.astype(bf16)
            send_total(k, n - 1)
        elif st < 2 * n:
            i = 2 * n - 1 - st
            cG[k, i + 1].wait_recv()
            send_total(k, i)
        else:
            cG[k, 0].wait_recv()
            for c in range(2):
                @pl.loop(0, Q // 32)
                def _(b):
                    x = tot[m, pl.ds(pl.multiple_of(b * 32, 32), 32), c * half + j * cw : c * half + (j + 1) * cw].astype(f32)
                    x = x * x
                    t = x[0:8] + x[8:16] + x[16:24] + x[24:32]
                    for q in range(cw // 128):
                        sq[:, q * 128 : (q + 1) * 128] += t[:, q * 128 : (q + 1) * 128]

    def send_total(k, i):
        m, j = k // SPLIT, k % SPLIT
        part = tot.at[m, pl.ds(off[i], sizes[i]), mycol(j)]
        to = partners[i - 1] if i else twin
        cG[k, i] = remote(part, part, gsem.at[0, k, i], gsem.at[1, k, i], rep=to)

    def vec_stage(t):
        if t < n:
            cV[t][0].wait_recv()
            vbuf[t + 1] = vbuf[t] + rV[t]
            if t < n - 1:
                cV[t + 1] = [remote(vbuf.at[t + 1], rV.at[t + 1], vsem.at[0, t + 1], vsem.at[1, t + 1], rep=partners[t])]
            else:
                cV[n] = [remote(vbuf.at[n], rV.at[n + d - 1], vsem.at[0, n + d - 1], vsem.at[1, n + d - 1], shard=zpeer[d]) for d in range(1, S)]
        elif t == n:
            total = vbuf[n]
            for d in range(1, S):
                cV[n][d - 1].wait_recv()
                total = total + rV[n + d - 1]
            vbuf[n + 1] = total

    sq[...] = jnp.zeros_like(sq)
    last = 2 * n
    for t in range(K + last):
        for st in range(last, -1, -1):
            k = t - st
            if 0 <= k < K:
                stage(k, st)
        vec_stage(t)

    sums = sq[:, 0:128]
    for q in range(1, cw // 128):
        sums = sums + sq[:, q * 128 : (q + 1) * 128]
    sqs[...] = sums
    cS = [remote(sqs, rS.at[d - 1], ssem.at[0, d - 1], ssem.at[1, d - 1], shard=zpeer[d]) for d in range(1, S)]
    for cp in ins:
        cp.wait()
    vt = vbuf[n + 1]
    vsq = jnp.sum(vt * vt, keepdims=True)
    for d in range(1, S):
        cS[d - 1].wait_recv()
        sums = sums + rS[d - 1]
    squares = jnp.sum(sums, keepdims=True) + vsq
    clip = jnp.minimum(1.0, 1.0 / jnp.sqrt(squares / count + 1e-06))
    clip_out[...] = jnp.broadcast_to(clip, clip_out.shape)

    def weights(m, rows, cols):
        return adam_piece(tot[m, rows, cols].astype(f32), bm[m, rows, cols], bo[m, rows, cols], bs[m, rows, cols], clip, decay_rate)[0].astype(bf16)

    wZ, wG = {}, {}
    for m in range(M):
        @pl.loop(0, pr // 16)
        def _(b):
            b16 = pl.multiple_of(b * 16, 16)
            wp[m, pl.ds(b16, 16), :] = weights(m, pl.ds(mul(off[n - 1] + b16, 16), 16), myhalf)

        for d in range(1, S):
            wZ[m, d] = remote(
                wp.at[m], wout.at[m, z, pl.ds(off[n - 1], pr), myhalf],
                wzsem.at[0, m, d - 1], wzsem.at[1, m, d - 1], shard=zpeer[d])
    mycols = pl.ds(pl.multiple_of(z * vmine.shape[1], 128), vmine.shape[1])
    vown = vbuf[n + 1, :, mycols]
    vtot[...] = vown
    vmine[...] = jnp.zeros_like(vmine)
    vmine[0:5, :] = adam_piece(vown[0:5], mv[...], ov[...], sv[...], clip, 0.0)[0]
    wV = [remote(vmine, vecw.at[:, mycols], wvsem.at[0, d - 1], wvsem.at[1, d - 1], shard=zpeer[d]) for d in range(1, S)]
    vecw[:, mycols] = vmine[...]

    outs = []
    for m in range(M):
        @pl.loop(0, Q // 16)
        def _(b):
            rows = pl.ds(pl.multiple_of(b * 16, 16), 16)
            wq[m, rows, :] = weights(m, rows, slice(None))
        cp = pltpu.make_async_copy(wq.at[m], wout.at[m, z], osem.at[m])
        cp.start()
        outs.append(cp)

    units = [(m, d) for m in range(M) for d in range(1, S)]

    def spread(u, st):
        m, d = units[u]
        if st == 0:
            wZ[m, d].wait_recv()
        else:
            wG[u, n - st].wait_recv()
        if st < n:
            i = n - 1 - st
            part = wout.at[m, zfrom[d], pl.ds(off[i], sizes[i]), myhalf]
            wG[u, i] = remote(part, part, wgsem.at[0, u, i], wgsem.at[1, u, i], rep=partners[i - 1] if i else twin)

    for t in range(len(units) + n):
        for st in range(n, -1, -1):
            u = t - st
            if 0 <= u < len(units):
                spread(u, st)
    for cp in wV:
        cp.wait_recv()
    for cp in outs:
        cp.wait()
    for cp in sends:
        cp.wait_send()


def body(
    R, S,
    grads_matrix,
    grads_vector,
    master_matrix,
    master_vector,
    moment_matrix,
    moment_vector,
    second_matrix,
    second_vector,
):
    f32, bf16 = jnp.float32, jnp.bfloat16
    M, D, W = grads_matrix.shape[2:]
    V = grads_vector.shape[2]
    Q = D // S
    n = int(math.log2(R))
    count = M * D * W + V * W
    half = W // 2
    cw = half // SPLIT
    K = M * SPLIT
    pr = Q >> (n - 1)
    U = M * (S - 1)
    dma = pltpu.SemaphoreType.DMA
    anyspec = pl.BlockSpec(memory_space=pl.ANY)
    vspec = pl.BlockSpec(memory_space=pltpu.VMEM)
    wout, tot, clip, vtot, vecw = pl.pallas_call(
        functools.partial(kernel, R, S, count),
        out_shape=(
            jax.ShapeDtypeStruct((M, S, Q, W), bf16),
            jax.ShapeDtypeStruct((M, Q, W), bf16),
            jax.ShapeDtypeStruct((8, 128), f32),
            jax.ShapeDtypeStruct((8, W // S), f32),
            jax.ShapeDtypeStruct((8, W), f32),
        ),
        in_specs=[anyspec, vspec, anyspec, vspec, anyspec, vspec, anyspec, vspec],
        out_specs=(anyspec, vspec, vspec, vspec, vspec),
        scratch_shapes=[
            pltpu.VMEM((K, S, Q, cw), bf16),
            pltpu.VMEM((K, S, Q, cw), bf16),
            [pltpu.VMEM((K, S, Q >> (i + 1), cw), bf16) for i in range(n - 1)],
            pltpu.VMEM((K, S - 1, pr, cw), bf16),
            pltpu.VMEM((M, pr, half), bf16),
            pltpu.VMEM((M, Q, W), bf16),
            pltpu.VMEM((n + 2, 8, W), f32),
            pltpu.VMEM((n + S - 1, 8, W), f32),
            pltpu.VMEM((8, cw), f32),
            pltpu.VMEM((8, 128), f32),
            pltpu.VMEM((S - 1, 8, 128), f32),
            pltpu.VMEM((8, W // S), f32),
            pltpu.VMEM((M, Q, W), f32),
            pltpu.VMEM((M, Q, W), f32),
            pltpu.VMEM((M, Q, W), f32),
            dma((K,)),
            dma((2, K)),
            dma((2, K, n - 1)),
            dma((2, K, S - 1)),
            dma((2, K, n)),
            dma((2, n + S - 1)),
            dma((2, S - 1)),
            dma((2, M, S - 1)),
            dma((2, U, n)),
            dma((2, S - 1)),
            dma((3,)),
            dma((M,)),
        ],
        compiler_params=pltpu.CompilerParams(
            collective_id=0, has_side_effects=True, vmem_limit_bytes=56 * 1024 * 1024
        ),
    )(
        grads_matrix.reshape(M, S, Q, W),
        grads_vector.reshape(V, W),
        master_matrix, master_vector, moment_matrix, moment_vector, second_matrix, second_vector,
    )
    factor = clip[0, 0]
    master_mat, moment_mat, second_mat = adam_piece(
        tot.astype(f32), master_matrix, moment_matrix, second_matrix, factor, decay_rate
    )
    master_vec, moment_vec, second_vec = adam_piece(
        vtot[:V], master_vector, moment_vector, second_vector, factor, 0.0
    )
    return (
        master_mat,
        master_vec,
        moment_mat,
        moment_vec,
        second_mat,
        second_vec,
        wout.reshape(M, D, W),
        vecw[:V].astype(bf16),
    )


def solution(mesh):
    R, S = mesh.shape["rep"], mesh.shape["shard"]
    return jax.shard_map(
        functools.partial(body, R, S),
        mesh=mesh,
        in_specs=(
            P("rep", "shard", None, None, None),
            P("rep", "shard", None, None),
            P(None, "shard", None),
            P(None, "shard"),
            P(None, "shard", None),
            P(None, "shard"),
            P(None, "shard", None),
            P(None, "shard"),
        ),
        out_specs=(
            P(None, "shard", None),
            P(None, "shard"),
            P(None, "shard", None),
            P(None, "shard"),
            P(None, "shard", None),
            P(None, "shard"),
            P(),
            P(),
        ),
        check_vma=False,
    )
```

```python
import functools
import math

import jax
import jax.numpy as jnp
from jax import lax
from jax.experimental import pallas as pl
from jax.experimental.pallas import tpu as pltpu
from jax.sharding import PartitionSpec as P

STEP = 1000


beta_first = 0.9
beta_second = 0.999
learn_rate = 0.01
decay_rate = 0.1
epsilon = 1e-08

SPLIT = 1


def adam_piece(total, master, moment, second, clip, decay):
    scaled = total * clip
    moment_next = beta_first * moment + (1.0 - beta_first) * scaled
    second_next = beta_second * second + (1.0 - beta_second) * scaled * scaled
    corrected = moment_next / (1.0 - beta_first**STEP)
    spread = jnp.sqrt(second_next / (1.0 - beta_second**STEP))
    update = corrected / (spread + epsilon)
    master_next = master - learn_rate * (update + decay * master)
    return (master_next, moment_next, second_next)


def kernel(
    R, S, count,
    gm, gv, mm, mv, om, ov, sm, sv,
    bm, bv, bo, bov, bs, bsv, wout, vout,
    tot, vecw, acc, rC, rX, rZ, wp, vbuf, rV, sq, sqs, rS, vmine,
    lsem, csem, xsem, zsem, gsem, vsem, ssem, wzsem, wgsem, wvsem, psem,
):
    f32, bf16 = jnp.float32, jnp.bfloat16
    n = int(math.log2(R))
    M, _, Q, W = gm.shape
    half = W // 2
    cw = half // SPLIT
    K = M * SPLIT
    r = lax.axis_index("rep")
    z = lax.axis_index("shard")
    core = r % 2
    bits, partners = [], []
    for i in range(n - 1):
        lo, hi = 2 << i, 1 << (n - 1 - i)
        mask = lo + core * (hi - lo)
        bit = (1 - core) * ((r // lo) % 2) + core * ((r // hi) % 2)
        bits.append(bit)
        partners.append(r + (1 - 2 * bit) * mask)
    twin = r + 1 - 2 * core
    sizes = [Q >> i for i in range(n)]
    offs = [0]
    for i in range(n - 1):
        offs.append(offs[-1] + bits[i] * sizes[i + 1])
    al = sizes[n - 1]
    pr = sizes[n - 1]

    def mul(x, m):
        return x if isinstance(x, int) else pl.multiple_of(x, m)

    off = [mul(o, al) for o in offs]
    mycol = lambda j: pl.ds(pl.multiple_of(core * half + j * cw, cw), cw)
    otcol = lambda j: pl.ds(pl.multiple_of((1 - core) * half + j * cw, cw), cw)
    myhalf = pl.ds(pl.multiple_of(core * half, half), half)
    zpeer = [lax.rem(z + d, S) for d in range(S)]
    zfrom = [lax.rem(z + S - d, S) for d in range(S)]

    sends = []

    def remote(src, dst, ss, rs, rep=None, shard=None):
        where = {"rep": rep} if shard is None else {"shard": shard}
        cp = pltpu.make_async_remote_copy(
            src_ref=src, dst_ref=dst, send_sem=ss, recv_sem=rs,
            device_id=where, device_id_type=pl.DeviceIdType.MESH,
        )
        cp.start()
        sends.append(cp)
        return cp

    barrier = pltpu.get_barrier_semaphore()
    for p in [twin] + partners:
        pl.semaphore_signal(barrier, inc=1, device_id={"rep": p}, device_id_type=pl.DeviceIdType.MESH)
    for d in range(1, S):
        pl.semaphore_signal(barrier, inc=1, device_id={"shard": zpeer[d]}, device_id_type=pl.DeviceIdType.MESH)

    locs = []
    for k in range(K):
        m, j = k // SPLIT, k % SPLIT
        cp = pltpu.make_async_copy(gm.at[m, :, :, mycol(j)], acc.at[k], lsem.at[k])
        cp.start()
        locs.append(cp)
    vbuf[...] = jnp.zeros_like(vbuf)
    vbuf[0, 0:5, :] = gv[...].astype(f32)
    pl.semaphore_wait(barrier, n + S - 1)

    cC = []
    for k in range(K):
        m, j = k // SPLIT, k % SPLIT
        cC.append(remote(gm.at[m, :, :, otcol(j)], rC.at[k], csem.at[0, k], csem.at[1, k], rep=twin))
    cV = {0: [remote(vbuf.at[0], rV.at[0], vsem.at[0, 0], vsem.at[1, 0], rep=twin)]}
    ins = []
    for i, (a, b) in enumerate(((mm, bm), (om, bo), (sm, bs))):
        cp = pltpu.make_async_copy(a, b, psem.at[i])
        cp.start()
        ins.append(cp)

    def add_rows(k, recv, start, size, base):
        step = min(size, 64)

        @pl.loop(0, S)
        def _(s):
            for b in range(size // step):
                rows = pl.ds(mul(start + b * step, 16), step)
                theirs = pl.ds(mul(start - base + b * step, 16), step)
                acc[k, s, rows, :] = (acc[k, s, rows, :].astype(f32) + recv[s, theirs, :].astype(f32)).astype(bf16)

    cX, cZ, cG = {}, {}, {}
    other = [mul(offs[i] + (1 - bits[i]) * sizes[i + 1], al) for i in range(n - 1)]

    def stage(k, st):
        m, j = k // SPLIT, k % SPLIT
        if st < n:
            if st == 0:
                locs[k].wait()
                cC[k].wait_recv()
                recv, base = rC.at[k], 0
            else:
                cX[k, st - 1].wait_recv()
                recv, base = rX[st - 1].at[k], offs[st]
            if st < n - 1:
                add_rows(k, recv, other[st], sizes[st + 1], base)
                cX[k, st] = remote(
                    acc.at[k, :, pl.ds(other[st], sizes[st + 1]), :], rX[st].at[k],
                    xsem.at[0, k, st], xsem.at[1, k, st], rep=partners[st])
                add_rows(k, recv, off[st + 1], sizes[st + 1], base)
            else:
                add_rows(k, recv, off[st], sizes[st], base)
                for d in range(1, S):
                    cZ[k, d] = remote(
                        acc.at[k, zpeer[d], pl.ds(off[st], pr), :], rZ.at[k, d - 1],
                        zsem.at[0, k, d - 1], zsem.at[1, k, d - 1], shard=zpeer[d])
        elif st == n:
            own = acc[k, z, pl.ds(off[n - 1], pr), :].astype(f32)
            for d in range(1, S):
                cZ[k, d].wait_recv()
                own = own + rZ[k, d - 1].astype(f32)
            tot[m, pl.ds(off[n - 1], pr), mycol(j)] = own.astype(bf16)
            send_total(k, n - 1)
        elif st < 2 * n:
            i = 2 * n - 1 - st
            cG[k, i + 1].wait_recv()
            send_total(k, i)
        else:
            cG[k, 0].wait_recv()
            for c in range(2):
                @pl.loop(0, Q // 32)
                def _(b):
                    x = tot[m, pl.ds(pl.multiple_of(b * 32, 32), 32), c * half + j * cw : c * half + (j + 1) * cw].astype(f32)
                    x = x * x
                    t = x[0:8] + x[8:16] + x[16:24] + x[24:32]
                    for q in range(cw // 128):
                        sq[:, q * 128 : (q + 1) * 128] += t[:, q * 128 : (q + 1) * 128]

    def send_total(k, i):
        m, j = k // SPLIT, k % SPLIT
        part = tot.at[m, pl.ds(off[i], sizes[i]), mycol(j)]
        to = partners[i - 1] if i else twin
        cG[k, i] = remote(part, part, gsem.at[0, k, i], gsem.at[1, k, i], rep=to)

    def vec_stage(t):
        if t < n:
            cV[t][0].wait_recv()
            vbuf[t + 1] = vbuf[t] + rV[t]
            if t < n - 1:
                cV[t + 1] = [remote(vbuf.at[t + 1], rV.at[t + 1], vsem.at[0, t + 1], vsem.at[1, t + 1], rep=partners[t])]
            else:
                cV[n] = [remote(vbuf.at[n], rV.at[n + d - 1], vsem.at[0, n + d - 1], vsem.at[1, n + d - 1], shard=zpeer[d]) for d in range(1, S)]
        elif t == n:
            total = vbuf[n]
            for d in range(1, S):
                cV[n][d - 1].wait_recv()
                total = total + rV[n + d - 1]
            vbuf[n + 1] = total

    sq[...] = jnp.zeros_like(sq)
    order = []
    for k in range(K):
        first = 8 * (k + 1)
        for st in range(2 * n + 1):
            order.append((0 if st == 0 else first + 5 * (st - 1), k, st))
    order += [(12 * t, K, t) for t in range(n + 1)]
    for _, k, st in sorted(order):
        if k < K:
            stage(k, st)
        else:
            vec_stage(st)

    sums = sq[:, 0:128]
    for q in range(1, cw // 128):
        sums = sums + sq[:, q * 128 : (q + 1) * 128]
    sqs[...] = sums
    cS = [remote(sqs, rS.at[d - 1], ssem.at[0, d - 1], ssem.at[1, d - 1], shard=zpeer[d]) for d in range(1, S)]
    for cp in ins:
        cp.wait()
    vt = vbuf[n + 1]
    vsq = jnp.sum(vt * vt, keepdims=True)
    for d in range(1, S):
        cS[d - 1].wait_recv()
        sums = sums + rS[d - 1]
    squares = jnp.sum(sums, keepdims=True) + vsq
    clip = jnp.minimum(1.0, 1.0 / jnp.sqrt(squares / count + 1e-06))

    def weights(m, rows, cols):
        return adam_piece(tot[m, rows, cols].astype(f32), bm[m, rows, cols], bo[m, rows, cols], bs[m, rows, cols], clip, decay_rate)[0].astype(bf16)

    wZ, wG = {}, {}
    for m in range(M):
        @pl.loop(0, pr // 16)
        def _(b):
            b16 = pl.multiple_of(b * 16, 16)
            wp[m, pl.ds(b16, 16), :] = weights(m, pl.ds(mul(off[n - 1] + b16, 16), 16), myhalf)

        for d in range(1, S):
            wZ[m, d] = remote(
                wp.at[m], wout.at[m, z, pl.ds(off[n - 1], pr), myhalf],
                wzsem.at[0, m, d - 1], wzsem.at[1, m, d - 1], shard=zpeer[d])
    mycols = pl.ds(pl.multiple_of(z * vmine.shape[1], 128), vmine.shape[1])
    vown = vbuf[n + 1, :, mycols]
    vmine[...] = jnp.zeros_like(vmine)
    bv[...], bov[...], bsv[...] = adam_piece(vown[0:5], mv[...], ov[...], sv[...], clip, 0.0)
    vmine[0:5, :] = bv[...]
    wV = [remote(vmine, vecw.at[:, mycols], wvsem.at[0, d - 1], wvsem.at[1, d - 1], shard=zpeer[d]) for d in range(1, S)]
    vecw[:, mycols] = vmine[...]

    def update(m):
        @pl.loop(0, Q // 16)
        def _(b):
            rows = pl.ds(pl.multiple_of(b * 16, 16), 16)
            one, two, three = adam_piece(
                tot[m, rows, :].astype(f32), bm[m, rows, :], bo[m, rows, :], bs[m, rows, :], clip, decay_rate)
            bm[m, rows, :], bo[m, rows, :], bs[m, rows, :] = one, two, three
            wout[m, z, rows, :] = one.astype(bf16)

    units = [(m, d) for m in range(M) for d in range(1, S)]

    def spread(u, st):
        m, d = units[u]
        if st == 0:
            wZ[m, d].wait_recv()
        else:
            wG[u, n - st].wait_recv()
        if st < n:
            i = n - 1 - st
            part = wout.at[m, zfrom[d], pl.ds(off[i], sizes[i]), myhalf]
            wG[u, i] = remote(part, part, wgsem.at[0, u, i], wgsem.at[1, u, i], rep=partners[i - 1] if i else twin)

    lag = [0, 2, 4, 5] if n == 3 else [2 * i for i in range(n + 1)]
    order = [(u + lag[st], -st, u) for u in range(len(units)) for st in range(n + 1)]
    order += [(2 * m + 1, -n - 1, m) for m in range(M)]
    for _, st, u in sorted(order):
        if st == -n - 1:
            update(u)
        else:
            spread(u, -st)
    for cp in wV:
        cp.wait_recv()
    vout[...] = vecw[0:5, :].astype(bf16)
    for cp in sends:
        cp.wait_send()


def body(
    R, S,
    grads_matrix,
    grads_vector,
    master_matrix,
    master_vector,
    moment_matrix,
    moment_vector,
    second_matrix,
    second_vector,
):
    f32, bf16 = jnp.float32, jnp.bfloat16
    M, D, W = grads_matrix.shape[2:]
    V = grads_vector.shape[2]
    Q = D // S
    n = int(math.log2(R))
    count = M * D * W + V * W
    half = W // 2
    cw = half // SPLIT
    K = M * SPLIT
    pr = Q >> (n - 1)
    U = M * (S - 1)
    dma = pltpu.SemaphoreType.DMA
    vspec = pl.BlockSpec(memory_space=pltpu.VMEM)
    hbm = pl.BlockSpec(memory_space=pltpu.HBM)
    mat = jax.ShapeDtypeStruct((M, Q, W), f32)
    vec = jax.ShapeDtypeStruct((V, W // S), f32)
    master_mat, master_vec, moment_mat, moment_vec, second_mat, second_vec, wout, vout = pl.pallas_call(
        functools.partial(kernel, R, S, count),
        out_shape=(
            mat, vec, mat, vec, mat, vec,
            jax.ShapeDtypeStruct((M, S, Q, W), bf16),
            jax.ShapeDtypeStruct((V, W), bf16),
        ),
        in_specs=[hbm, vspec, hbm, vspec, hbm, vspec, hbm, vspec],
        out_specs=(vspec,) * 8,
        scratch_shapes=[
            pltpu.VMEM((M, Q, W), bf16),
            pltpu.VMEM((8, W), f32),
            pltpu.VMEM((K, S, Q, cw), bf16),
            pltpu.VMEM((K, S, Q, cw), bf16),
            [pltpu.VMEM((K, S, Q >> (i + 1), cw), bf16) for i in range(n - 1)],
            pltpu.VMEM((K, S - 1, pr, cw), bf16),
            pltpu.VMEM((M, pr, half), bf16),
            pltpu.VMEM((n + 2, 8, W), f32),
            pltpu.VMEM((n + S - 1, 8, W), f32),
            pltpu.VMEM((8, cw), f32),
            pltpu.VMEM((8, 128), f32),
            pltpu.VMEM((S - 1, 8, 128), f32),
            pltpu.VMEM((8, W // S), f32),
            dma((K,)),
            dma((2, K)),
            dma((2, K, n - 1)),
            dma((2, K, S - 1)),
            dma((2, K, n)),
            dma((2, n + S - 1)),
            dma((2, S - 1)),
            dma((2, M, S - 1)),
            dma((2, U, n)),
            dma((2, S - 1)),
            dma((3,)),
        ],
        compiler_params=pltpu.CompilerParams(
            collective_id=0, has_side_effects=True, vmem_limit_bytes=44 * 1024 * 1024
        ),
    )(
        grads_matrix.reshape(M, S, Q, W),
        grads_vector.reshape(V, W),
        master_matrix, master_vector, moment_matrix, moment_vector, second_matrix, second_vector,
    )
    return (
        master_mat,
        master_vec,
        moment_mat,
        moment_vec,
        second_mat,
        second_vec,
        wout.reshape(M, D, W),
        vout,
    )


def solution(mesh):
    R, S = mesh.shape["rep"], mesh.shape["shard"]
    return jax.shard_map(
        functools.partial(body, R, S),
        mesh=mesh,
        in_specs=(
            P("rep", "shard", None, None, None),
            P("rep", "shard", None, None),
            P(None, "shard", None),
            P(None, "shard"),
            P(None, "shard", None),
            P(None, "shard"),
            P(None, "shard", None),
            P(None, "shard"),
        ),
        out_specs=(
            P(None, "shard", None),
            P(None, "shard"),
            P(None, "shard", None),
            P(None, "shard"),
            P(None, "shard", None),
            P(None, "shard"),
            P(),
            P(),
        ),
        check_vma=False,
    )
```

```python
import functools
import math

import jax
import jax.numpy as jnp
from jax import lax
from jax.experimental import pallas as pl
from jax.experimental.pallas import tpu as pltpu
from jax.sharding import PartitionSpec as P

STEP = 1000


beta_first = 0.9
beta_second = 0.999
learn_rate = 0.01
decay_rate = 0.1
epsilon = 1e-08

SPLIT = 1


def adam_piece(total, master, moment, second, clip, decay):
    scaled = total * clip
    moment_next = beta_first * moment + (1.0 - beta_first) * scaled
    second_next = beta_second * second + (1.0 - beta_second) * scaled * scaled
    corrected = moment_next / (1.0 - beta_first**STEP)
    spread = jnp.sqrt(second_next / (1.0 - beta_second**STEP))
    update = corrected / (spread + epsilon)
    master_next = master - learn_rate * (update + decay * master)
    return (master_next, moment_next, second_next)


def kernel(
    R, S, count,
    gm, gv, mm, mv, om, ov, sm, sv,
    bm, bv, bo, bov, bs, bsv, wout, vout,
    tot, vecw, acc, rC, rX, rZ, wp, wq, vbuf, rV, sq, sqs, rS, vmine,
    lsem, csem, xsem, zsem, gsem, vsem, ssem, wzsem, wgsem, wvsem, psem, osem,
):
    f32, bf16 = jnp.float32, jnp.bfloat16
    n = int(math.log2(R))
    M, _, Q, W = gm.shape
    half = W // 2
    cw = half // SPLIT
    K = M * SPLIT
    r = lax.axis_index("rep")
    z = lax.axis_index("shard")
    core = r % 2
    bits, partners = [], []
    for i in range(n - 1):
        lo, hi = 2 << i, 1 << (n - 1 - i)
        mask = lo + core * (hi - lo)
        bit = (1 - core) * ((r // lo) % 2) + core * ((r // hi) % 2)
        bits.append(bit)
        partners.append(r + (1 - 2 * bit) * mask)
    twin = r + 1 - 2 * core
    sizes = [Q >> i for i in range(n)]
    offs = [0]
    for i in range(n - 1):
        offs.append(offs[-1] + bits[i] * sizes[i + 1])
    al = sizes[n - 1]
    pr = sizes[n - 1]

    def mul(x, m):
        return x if isinstance(x, int) else pl.multiple_of(x, m)

    off = [mul(o, al) for o in offs]
    mycol = lambda j: pl.ds(pl.multiple_of(core * half + j * cw, cw), cw)
    otcol = lambda j: pl.ds(pl.multiple_of((1 - core) * half + j * cw, cw), cw)
    myhalf = pl.ds(pl.multiple_of(core * half, half), half)
    zpeer = [lax.rem(z + d, S) for d in range(S)]
    zfrom = [lax.rem(z + S - d, S) for d in range(S)]

    sends = []

    def remote(src, dst, ss, rs, rep=None, shard=None):
        where = {"rep": rep} if shard is None else {"shard": shard}
        cp = pltpu.make_async_remote_copy(
            src_ref=src, dst_ref=dst, send_sem=ss, recv_sem=rs,
            device_id=where, device_id_type=pl.DeviceIdType.MESH,
        )
        cp.start()
        sends.append(cp)
        return cp

    barrier = pltpu.get_barrier_semaphore()
    for p in [twin] + partners:
        pl.semaphore_signal(barrier, inc=1, device_id={"rep": p}, device_id_type=pl.DeviceIdType.MESH)
    for d in range(1, S):
        pl.semaphore_signal(barrier, inc=1, device_id={"shard": zpeer[d]}, device_id_type=pl.DeviceIdType.MESH)

    locs = []
    for k in range(K):
        m, j = k // SPLIT, k % SPLIT
        cp = pltpu.make_async_copy(gm.at[m, :, :, mycol(j)], acc.at[k], lsem.at[k])
        cp.start()
        locs.append(cp)
    vbuf[...] = jnp.zeros_like(vbuf)
    vbuf[0, 0:5, :] = gv[...].astype(f32)
    pl.semaphore_wait(barrier, n + S - 1)

    cV = {0: [remote(vbuf.at[0], rV.at[0], vsem.at[0, 0], vsem.at[1, 0], rep=twin)]}
    cC = []
    for k in range(K):
        m, j = k // SPLIT, k % SPLIT
        cC.append(remote(gm.at[m, :, :, otcol(j)], rC.at[k], csem.at[0, k], csem.at[1, k], rep=twin))
    ins = []
    for i, (a, b) in enumerate(((mm, bm), (om, bo), (sm, bs))):
        cp = pltpu.make_async_copy(a, b, psem.at[i])
        cp.start()
        ins.append(cp)

    def add_rows(k, recv, start, size, base):
        step = min(size, 64)

        @pl.loop(0, S)
        def _(s):
            for b in range(size // step):
                rows = pl.ds(mul(start + b * step, 16), step)
                theirs = pl.ds(mul(start - base + b * step, 16), step)
                acc[k, s, rows, :] = (acc[k, s, rows, :].astype(f32) + recv[s, theirs, :].astype(f32)).astype(bf16)

    cX, cZ, cG = {}, {}, {}
    other = [mul(offs[i] + (1 - bits[i]) * sizes[i + 1], al) for i in range(n - 1)]

    def stage(k, st):
        m, j = k // SPLIT, k % SPLIT
        if st < n:
            if st == 0:
                locs[k].wait()
                cC[k].wait_recv()
                recv, base = rC.at[k], 0
            else:
                cX[k, st - 1].wait_recv()
                recv, base = rX[st - 1].at[k], offs[st]
            if st < n - 1:
                add_rows(k, recv, other[st], sizes[st + 1], base)
                cX[k, st] = remote(
                    acc.at[k, :, pl.ds(other[st], sizes[st + 1]), :], rX[st].at[k],
                    xsem.at[0, k, st], xsem.at[1, k, st], rep=partners[st])
                add_rows(k, recv, off[st + 1], sizes[st + 1], base)
            else:
                add_rows(k, recv, off[st], sizes[st], base)
                for d in range(1, S):
                    cZ[k, d] = remote(
                        acc.at[k, zpeer[d], pl.ds(off[st], pr), :], rZ.at[k, d - 1],
                        zsem.at[0, k, d - 1], zsem.at[1, k, d - 1], shard=zpeer[d])
        elif st == n:
            own = acc[k, z, pl.ds(off[n - 1], pr), :].astype(f32)
            for d in range(1, S):
                cZ[k, d].wait_recv()
                own = own + rZ[k, d - 1].astype(f32)
            tot[m, pl.ds(off[n - 1], pr), mycol(j)] = own.astype(bf16)
            send_total(k, n - 1)
        elif st < 2 * n:
            i = 2 * n - 1 - st
            cG[k, i + 1].wait_recv()
            send_total(k, i)
        else:
            cG[k, 0].wait_recv()
            for c in range(2):
                @pl.loop(0, Q // 32)
                def _(b):
                    x = tot[m, pl.ds(pl.multiple_of(b * 32, 32), 32), c * half + j * cw : c * half + (j + 1) * cw].astype(f32)
                    x = x * x
                    t = x[0:8] + x[8:16] + x[16:24] + x[24:32]
                    for q in range(cw // 128):
                        sq[:, q * 128 : (q + 1) * 128] += t[:, q * 128 : (q + 1) * 128]

    def send_total(k, i):
        m, j = k // SPLIT, k % SPLIT
        part = tot.at[m, pl.ds(off[i], sizes[i]), mycol(j)]
        to = partners[i - 1] if i else twin
        cG[k, i] = remote(part, part, gsem.at[0, k, i], gsem.at[1, k, i], rep=to)

    def vec_stage(t):
        if t < n:
            cV[t][0].wait_recv()
            vbuf[t + 1] = vbuf[t] + rV[t]
            if t < n - 1:
                cV[t + 1] = [remote(vbuf.at[t + 1], rV.at[t + 1], vsem.at[0, t + 1], vsem.at[1, t + 1], rep=partners[t])]
            else:
                cV[n] = [remote(vbuf.at[n], rV.at[n + d - 1], vsem.at[0, n + d - 1], vsem.at[1, n + d - 1], shard=zpeer[d]) for d in range(1, S)]
        elif t == n:
            total = vbuf[n]
            for d in range(1, S):
                cV[n][d - 1].wait_recv()
                total = total + rV[n + d - 1]
            vbuf[n + 1] = total

    sq[...] = jnp.zeros_like(sq)
    order = []
    for k in range(K):
        first = 8 * (k + 1)
        for st in range(2 * n + 1):
            order.append((0 if st == 0 else first + 8 * (st - 1), k, st))
    order += [(-1 if t == 0 else 1 if t == 1 else 7 * t, K, t) for t in range(n + 1)]
    for _, k, st in sorted(order):
        if k < K:
            stage(k, st)
        else:
            vec_stage(st)

    sums = sq[:, 0:128]
    for q in range(1, cw // 128):
        sums = sums + sq[:, q * 128 : (q + 1) * 128]
    sqs[...] = sums
    cS = [remote(sqs, rS.at[d - 1], ssem.at[0, d - 1], ssem.at[1, d - 1], shard=zpeer[d]) for d in range(1, S)]
    for cp in ins:
        cp.wait()
    vt = vbuf[n + 1]
    vsq = jnp.sum(vt * vt, keepdims=True)
    for d in range(1, S):
        cS[d - 1].wait_recv()
        sums = sums + rS[d - 1]
    squares = jnp.sum(sums, keepdims=True) + vsq
    clip = jnp.minimum(1.0, 1.0 / jnp.sqrt(squares / count + 1e-06))

    def weights(m, rows, cols):
        return adam_piece(tot[m, rows, cols].astype(f32), bm[m, rows, cols], bo[m, rows, cols], bs[m, rows, cols], clip, decay_rate)[0].astype(bf16)

    wZ, wG = {}, {}
    for m in range(M):
        @pl.loop(0, pr // 16)
        def _(b):
            b16 = pl.multiple_of(b * 16, 16)
            wp[m, pl.ds(b16, 16), :] = weights(m, pl.ds(mul(off[n - 1] + b16, 16), 16), myhalf)

        for d in range(1, S):
            wZ[m, d] = remote(
                wp.at[m], wout.at[m, z, pl.ds(off[n - 1], pr), myhalf],
                wzsem.at[0, m, d - 1], wzsem.at[1, m, d - 1], shard=zpeer[d])
    mycols = pl.ds(pl.multiple_of(z * vmine.shape[1], 128), vmine.shape[1])
    vown = vbuf[n + 1, :, mycols]
    vmine[...] = jnp.zeros_like(vmine)
    bv[...], bov[...], bsv[...] = adam_piece(vown[0:5], mv[...], ov[...], sv[...], clip, 0.0)
    vmine[0:5, :] = bv[...]
    wV = [remote(vmine, vecw.at[:, mycols], wvsem.at[0, d - 1], wvsem.at[1, d - 1], shard=zpeer[d]) for d in range(1, S)]
    vecw[:, mycols] = vmine[...]

    outs = []

    def update(m):
        @pl.loop(0, Q // 16)
        def _(b):
            rows = pl.ds(pl.multiple_of(b * 16, 16), 16)
            one, two, three = adam_piece(
                tot[m, rows, :].astype(f32), bm[m, rows, :], bo[m, rows, :], bs[m, rows, :], clip, decay_rate)
            bm[m, rows, :], bo[m, rows, :], bs[m, rows, :] = one, two, three
            wq[m, rows, :] = one.astype(bf16)

        cp = pltpu.make_async_copy(wq.at[m], wout.at[m, z], osem.at[m])
        cp.start()
        outs.append(cp)

    units = [(m, d) for m in range(M) for d in range(1, S)]

    def spread(u, st):
        m, d = units[u]
        if st == 0:
            wZ[m, d].wait_recv()
        else:
            wG[u, n - st].wait_recv()
        if st < n:
            i = n - 1 - st
            part = wout.at[m, zfrom[d], pl.ds(off[i], sizes[i]), myhalf]
            wG[u, i] = remote(part, part, wgsem.at[0, u, i], wgsem.at[1, u, i], rep=partners[i - 1] if i else twin)

    lag = [0, 3, 6, 7] if n == 3 else [2 * i for i in range(n + 1)]
    order = [(u + lag[st], -st, u) for u in range(len(units)) for st in range(n + 1)]
    order += [(4 * m + 2, -n - 1, m) for m in range(M)]
    for _, st, u in sorted(order):
        if st == -n - 1:
            update(u)
        else:
            spread(u, -st)
    for cp in wV:
        cp.wait_recv()
    for cp in outs:
        cp.wait()
    vout[...] = vecw[0:5, :].astype(bf16)
    for cp in sends:
        cp.wait_send()


def body(
    R, S,
    grads_matrix,
    grads_vector,
    master_matrix,
    master_vector,
    moment_matrix,
    moment_vector,
    second_matrix,
    second_vector,
):
    f32, bf16 = jnp.float32, jnp.bfloat16
    M, D, W = grads_matrix.shape[2:]
    V = grads_vector.shape[2]
    Q = D // S
    n = int(math.log2(R))
    count = M * D * W + V * W
    half = W // 2
    cw = half // SPLIT
    K = M * SPLIT
    pr = Q >> (n - 1)
    U = M * (S - 1)
    dma = pltpu.SemaphoreType.DMA
    vspec = pl.BlockSpec(memory_space=pltpu.VMEM)
    hbm = pl.BlockSpec(memory_space=pltpu.HBM)
    mat = jax.ShapeDtypeStruct((M, Q, W), f32)
    vec = jax.ShapeDtypeStruct((V, W // S), f32)
    master_mat, master_vec, moment_mat, moment_vec, second_mat, second_vec, wout, vout = pl.pallas_call(
        functools.partial(kernel, R, S, count),
        out_shape=(
            mat, vec, mat, vec, mat, vec,
            jax.ShapeDtypeStruct((M, S, Q, W), bf16),
            jax.ShapeDtypeStruct((V, W), bf16),
        ),
        in_specs=[hbm, vspec, hbm, vspec, hbm, vspec, hbm, vspec],
        out_specs=(vspec,) * 6 + (hbm, vspec),
        scratch_shapes=[
            pltpu.VMEM((M, Q, W), bf16),
            pltpu.VMEM((8, W), f32),
            pltpu.VMEM((K, S, Q, cw), bf16),
            pltpu.VMEM((K, S, Q, cw), bf16),
            [pltpu.VMEM((K, S, Q >> (i + 1), cw), bf16) for i in range(n - 1)],
            pltpu.VMEM((K, S - 1, pr, cw), bf16),
            pltpu.VMEM((M, pr, half), bf16),
            pltpu.VMEM((M, Q, W), bf16),
            pltpu.VMEM((n + 2, 8, W), f32),
            pltpu.VMEM((n + S - 1, 8, W), f32),
            pltpu.VMEM((8, cw), f32),
            pltpu.VMEM((8, 128), f32),
            pltpu.VMEM((S - 1, 8, 128), f32),
            pltpu.VMEM((8, W // S), f32),
            dma((K,)),
            dma((2, K)),
            dma((2, K, n - 1)),
            dma((2, K, S - 1)),
            dma((2, K, n)),
            dma((2, n + S - 1)),
            dma((2, S - 1)),
            dma((2, M, S - 1)),
            dma((2, U, n)),
            dma((2, S - 1)),
            dma((3,)),
            dma((M,)),
        ],
        compiler_params=pltpu.CompilerParams(
            collective_id=0, has_side_effects=True, vmem_limit_bytes=44 * 1024 * 1024
        ),
    )(
        grads_matrix.reshape(M, S, Q, W),
        grads_vector.reshape(V, W),
        master_matrix, master_vector, moment_matrix, moment_vector, second_matrix, second_vector,
    )
    return (
        master_mat,
        master_vec,
        moment_mat,
        moment_vec,
        second_mat,
        second_vec,
        wout.reshape(M, D, W),
        vout,
    )


def solution(mesh):
    R, S = mesh.shape["rep"], mesh.shape["shard"]
    return jax.shard_map(
        functools.partial(body, R, S),
        mesh=mesh,
        in_specs=(
            P("rep", "shard", None, None, None),
            P("rep", "shard", None, None),
            P(None, "shard", None),
            P(None, "shard"),
            P(None, "shard", None),
            P(None, "shard"),
            P(None, "shard", None),
            P(None, "shard"),
        ),
        out_specs=(
            P(None, "shard", None),
            P(None, "shard"),
            P(None, "shard", None),
            P(None, "shard"),
            P(None, "shard", None),
            P(None, "shard"),
            P(),
            P(),
        ),
        check_vma=False,
    )
```
